32 devices in a mesh: grp: 2 (over x), slab: 16 (over z, y, core).
Axes of the slice: x: 2, y: 2, z: 4, core: 2. Of those that a mesh axis runs over, the one named last changes fastest.
Arguments:
- courant: float32 [64, 64, 256], P(('grp', 'slab')), parts along dimension 0, may hold values from 0.08 to 0.28
- wave_level: float32 [64, 64, 256], P(('grp', 'slab')), parts along dimension 0, may hold values from -6 to 6
- wave_above: float32 [64, 64, 256], P(('grp', 'slab')), parts along dimension 0, may hold values from -6 to 6
- adjoint_level: float32 [64, 64, 256], P(('grp', 'slab')), parts along dimension 0, may hold values from -6 to 6
- adjoint_above: float32 [64, 64, 256], P(('grp', 'slab')), parts along dimension 0, may hold values from -6 to 6
- residual_data: float32 [8, 2048], P(None, 'grp'), parts along dimension 1, may hold values from -6 to 6
- wavelet: float32 [512], P('grp'), parts along dimension 0, may hold values from -6 to 6
- checkpoint_step: int32 [2], P('grp'), parts along dimension 0, may hold values from 0 to 248
- source_cells: int32 [3, 512], P(None, 'grp'), parts along dimension 1, may hold values from 0 to 255, as said below
- receiver_cells: int32 [3, 2048], P(None, 'grp'), parts along dimension 1, may hold values from 0 to 255, as said below
- conv_weight: bfloat16 [54, 32], replicated, may hold values from -0.875 to 0.875
- conv_bias: float32 [32], replicated, may hold values from -4 to 4
- mix_weight: bfloat16 [32, 32], replicated, may hold values from -1 to 1
- mix_bias: float32 [32], replicated, may hold values from -4 to 4
- out_weight: bfloat16 [32], replicated, may hold values from -1 to 1
- update_cotangent: bfloat16 [64, 64, 256], P(('grp', 'slab')), parts along dimension 0, may hold values from -6 to 6
Outputs:
- gradient_image: float32 [64, 64, 256], P(('grp', 'slab')), parts along dimension 0
- adjoint_first: float32 [64, 64, 256], P(('grp', 'slab')), parts along dimension 0
- adjoint_second: float32 [64, 64, 256], P(('grp', 'slab')), parts along dimension 0
- input_gradient: float32 [64, 64, 256], P(('grp', 'slab')), parts along dimension 0
- grad_conv: float32 [108, 32], P('grp'), parts along dimension 0
- grad_conv_bias: float32 [64], P('grp'), parts along dimension 0
- grad_mix: float32 [64, 32], P('grp'), parts along dimension 0
- grad_mix_bias: float32 [64], P('grp'), parts along dimension 0
- grad_out: float32 [64], P('grp'), parts along dimension 0
The draws below stay inside these ranges and needn't reach their ends.
There are 2 independent parts, one for each index of `grp`. The reference program is written for one: setup_inputs(seed, part) draws one part's arguments, and reference() takes and returns one part's arrays. A program takes and returns all parts, laid end to end along the dimension named above; an argument that names none is the same for every part. Nothing has to cross between parts.
Inputs may be any that keep to these rules, and one draw needn't show every extreme that they name: `source_cells`: row 0 is a cell index along the first grid dimension (below 32), row 1 along the second (below 64), row 2 along the third (below 256); elements may share a cell. `receiver_cells`: row 0 is a cell index along the first grid dimension (below 32), row 1 along the second (below 64), row 2 along the third (below 256); receivers may share a cell.
All inputs are finite; a program needn't handle non-finite values.
Results may differ from the reference program's by a relative error of at most 0.009.
The reference program's roundings to bfloat16 on the way (of `cnn_input`, `patches`, `act_one`, `act_two`, `grad_pre_two` and `grad_pre_one`) count: a program that leaves them out, or rounds other values in their place, can miss the bound.
Values may be sent and summed in bfloat16 or wider, within the bound.
A program may use at most 128 MiB of HBM per device.

```python
import jax
import jax.numpy as jnp
from jax import lax

CZ = 2
NX = 64
NY = 256
NSTEP = 8
NT = 256
NSRC = 256
NREC = 1024
CH = 32
TAPS = 54
NZ = 32


def draw_cells(key, how_many):
    subkeys = jax.random.split(key, 3)
    depth_cells = jax.random.randint(subkeys[0], (how_many,), 0, NZ)
    row_cells = jax.random.randint(subkeys[1], (how_many,), 0, NX)
    column_cells = jax.random.randint(subkeys[2], (how_many,), 0, NY)
    cell_table = jnp.stack([depth_cells, row_cells, column_cells]).astype(jnp.int32)
    cell_table = cell_table.at[:, 0].set(jnp.array([NZ - 1, NX - 1, NY - 1], jnp.int32))
    return cell_table.at[:, 1].set(0)


def draw_source_cells(key, part):
    key = jax.random.fold_in(key, 11)
    return draw_cells(key, NSRC)


def draw_receiver_cells(key, part):
    key = jax.random.fold_in(key, 23)
    return draw_cells(key, NREC)


def steps_of(own_key, extent, cuts, least, high):
    def one(dim, blocks):
        draws = jax.random.uniform(jax.random.fold_in(jax.random.fold_in(own_key, 6), dim), (blocks,), jnp.float32, least / len(cuts), high / len(cuts))
        return jnp.repeat(jnp.exp(draws), extent[dim] // blocks).reshape((-1,) + (1,) * (len(extent) - dim - 1))

    gain = one(*cuts[0])
    for cut in cuts[1:]:
        gain = gain * one(*cut)
    return gain


def bell_draw(key, dims, spread, reach, cuts=(), kind=jnp.bfloat16):
    loudness = steps_of(key, dims, cuts, -0.22, 0.18) if cuts else 1.0
    entries = jax.random.normal(key, dims, jnp.float32) * spread * loudness
    return jnp.minimum(jnp.maximum(entries, -reach), reach).astype(kind)


def setup_inputs(seed: int = 0, part: int = 0) -> dict:
    streams_of = jax.random.split(jax.random.key(seed), 17)
    own_keys = jax.random.split(jax.random.fold_in(streams_of[16], part), 17)
    return {
        "courant": jnp.clip(0.08 + 0.2 * jax.random.uniform(own_keys[0], (NZ, NX, NY), jnp.float32) ** steps_of(own_keys[0], (NZ, NX, NY), ((0, 16),), -0.2, 0.2), 0.08, 0.28),
        "wave_level": bell_draw(own_keys[1], (NZ, NX, NY), 1.0, 6.0, ((0, 16),), jnp.float32),
        "wave_above": bell_draw(own_keys[2], (NZ, NX, NY), 1.0, 6.0, ((0, 16),), jnp.float32),
        "adjoint_level": bell_draw(own_keys[3], (NZ, NX, NY), 1.0, 6.0, ((0, 16),), jnp.float32),
        "adjoint_above": bell_draw(own_keys[4], (NZ, NX, NY), 1.0, 6.0, ((0, 16),), jnp.float32),
        "residual_data": bell_draw(own_keys[5], (NSTEP, NREC), 1.0, 6.0, (), jnp.float32),
        "wavelet": bell_draw(own_keys[6], (NT,), 1.0, 6.0, (), jnp.float32),
        "checkpoint_step": jax.random.randint(own_keys[7], (1,), 0, NT - NSTEP + 1).astype(jnp.int32),
        "source_cells": draw_source_cells(jax.random.fold_in(jax.random.fold_in(streams_of[16], part), 71), part),
        "receiver_cells": draw_receiver_cells(jax.random.fold_in(jax.random.fold_in(streams_of[16], part), 71), part),
        "conv_weight": bell_draw(streams_of[10], (TAPS, CH), TAPS ** -0.5, 0.875),
        "conv_bias": bell_draw(streams_of[11], (CH,), 1.0, 4.0, (), jnp.float32),
        "mix_weight": bell_draw(streams_of[12], (CH, CH), CH ** -0.5, 1.0),
        "mix_bias": bell_draw(streams_of[13], (CH,), 1.0, 4.0, (), jnp.float32),
        "out_weight": bell_draw(streams_of[14], (CH,), CH ** -0.5, 1.0),
        "update_cotangent": bell_draw(own_keys[15], (NZ, NX, NY), 1.0, 6.0, ((0, 16),)),
    }


def laplace(volume):
    padded = jnp.pad(volume, 1)
    return (padded[2:, 1:-1, 1:-1] + padded[:-2, 1:-1, 1:-1] + padded[1:-1, 2:, 1:-1]
            + padded[1:-1, :-2, 1:-1] + padded[1:-1, 1:-1, 2:] + padded[1:-1, 1:-1, :-2] - 6.0 * volume)


def silu_slope(values):
    sigmoid_part = jax.nn.sigmoid(values)
    return sigmoid_part * (1.0 + values * (1.0 - sigmoid_part))


def make_patches(window):
    planes = window.shape[1] - 2
    rows_all = window.shape[2] - 2
    cols_all = window.shape[3] - 2
    pieces = []
    for channel in range(2):
        for shift_z in range(3):
            for shift_x in range(3):
                for shift_y in range(3):
                    pieces.append(window[channel, shift_z:shift_z + planes, shift_x:shift_x + rows_all, shift_y:shift_y + cols_all])
    return jnp.stack(pieces)


def spread_taps(tap_fields):
    padded = jnp.pad(tap_fields, ((0, 0), (0, 0), (1, 1), (1, 1)))
    rows_all = tap_fields.shape[2]
    cols_all = tap_fields.shape[3]
    spreads = []
    for shift_z in range(3):
        running = jnp.zeros(tap_fields.shape[1:], jnp.float32)
        for shift_x in range(3):
            for shift_y in range(3):
                tap_index = 9 * shift_z + 3 * shift_x + shift_y
                running = running + padded[tap_index, :, 2 - shift_x:2 - shift_x + rows_all, 2 - shift_y:2 - shift_y + cols_all]
        spreads.append(running)
    return jnp.stack(spreads)


def network_block(patches, cotangent, conv_weight, conv_bias, mix_weight, mix_bias, out_weight):
    floats = jnp.float32
    highest = lax.Precision.HIGHEST
    pre_one = jnp.einsum("kc,kzxy->czxy", conv_weight.astype(floats), patches.astype(floats), precision=highest) + conv_bias[:, None, None, None]
    act_one = jax.nn.silu(pre_one).astype(jnp.bfloat16)
    pre_two = jnp.einsum("dc,dzxy->czxy", mix_weight.astype(floats), act_one.astype(floats), precision=highest) + mix_bias[:, None, None, None]
    act_two = jax.nn.silu(pre_two).astype(jnp.bfloat16)
    cot_two = out_weight.astype(floats)[:, None, None, None] * cotangent.astype(floats)[None]
    grad_pre_two = (cot_two * silu_slope(pre_two)).astype(jnp.bfloat16)
    grad_out = jnp.einsum("czxy,zxy->c", act_two.astype(floats), cotangent.astype(floats), precision=highest)
    grad_mix_bias = jnp.sum(grad_pre_two.astype(floats), axis=(1, 2, 3))
    grad_mix = jnp.einsum("dzxy,czxy->dc", act_one.astype(floats), grad_pre_two.astype(floats), precision=highest)
    cot_one = jnp.einsum("dc,czxy->dzxy", mix_weight.astype(floats), grad_pre_two.astype(floats), precision=highest)
    grad_pre_one = (cot_one * silu_slope(pre_one)).astype(jnp.bfloat16)
    grad_conv_bias = jnp.sum(grad_pre_one.astype(floats), axis=(1, 2, 3))
    grad_conv = jnp.einsum("kzxy,czxy->kc", patches.astype(floats), grad_pre_one.astype(floats), precision=highest)
    tap_fields = jnp.einsum("tc,czxy->tzxy", conv_weight[:TAPS // 2].astype(floats), grad_pre_one.astype(floats), precision=highest)
    return (grad_conv, grad_conv_bias, grad_mix, grad_mix_bias, grad_out), tap_fields


def reference(courant, wave_level, wave_above, adjoint_level, adjoint_above, residual_data, wavelet, checkpoint_step, source_cells, receiver_cells, conv_weight, conv_bias, mix_weight, mix_bias, out_weight, update_cotangent):
    image_sum = jnp.zeros_like(courant)
    current, upper_wave = wave_level, wave_above
    adjoint, upper_adjoint = adjoint_level, adjoint_above
    for turn_index in range(NSTEP):
        level_now = NSTEP - turn_index
        lap_wave = laplace(current)
        image_sum = image_sum + adjoint * lap_wave
        pulse_value = lax.dynamic_slice_in_dim(wavelet, checkpoint_step[0] + (level_now - 1), 1)
        sources = jnp.zeros_like(current).at[source_cells[0], source_cells[1], source_cells[2]].add(jnp.broadcast_to(pulse_value, (NSRC,)))
        records = jnp.zeros_like(current).at[receiver_cells[0], receiver_cells[1], receiver_cells[2]].add(residual_data[level_now - 1])
        lower_wave = 2.0 * current - upper_wave + courant * lap_wave + sources
        lower_adjoint = 2.0 * adjoint - upper_adjoint + laplace(courant * adjoint) + records
        upper_wave, current = current, lower_wave
        upper_adjoint, adjoint = adjoint, lower_adjoint
    cnn_input = jnp.stack([image_sum, courant]).astype(jnp.bfloat16)
    padded = jnp.pad(cnn_input, ((0, 0), (1, 1), (1, 1), (1, 1)))
    block_count = NZ // CZ
    zero_grads = (jnp.zeros((TAPS, CH), jnp.float32), jnp.zeros((CH,), jnp.float32), jnp.zeros((CH, CH), jnp.float32),
                  jnp.zeros((CH,), jnp.float32), jnp.zeros((CH,), jnp.float32))

    def block_step(carried, block_index):
        start_plane = (block_index * CZ).astype(jnp.int32)
        window = lax.dynamic_slice_in_dim(padded, start_plane, CZ + 2, 1)
        cotangent = lax.dynamic_slice_in_dim(update_cotangent, start_plane, CZ, 0)
        block_grads, tap_fields = network_block(make_patches(window), cotangent, conv_weight, conv_bias, mix_weight, mix_bias, out_weight)
        summed = tuple(earlier + addend for earlier, addend in zip(carried, block_grads))
        return summed, spread_taps(tap_fields)

    summed, spreads = lax.scan(block_step, zero_grads, jnp.arange(block_count, dtype=jnp.int32))
    spreads = jnp.moveaxis(spreads, 1, 0).reshape(3, NZ, NX, NY)
    padded_spreads = jnp.pad(spreads, ((0, 0), (1, 1), (0, 0), (0, 0)))
    input_gradient = spreads[1] + padded_spreads[2, :NZ] + padded_spreads[0, 2:]
    grad_scale = float(NZ * NX * NY) ** -0.5
    return (image_sum, adjoint, upper_adjoint, input_gradient, summed[0] * grad_scale, summed[1] * grad_scale,
            summed[2] * grad_scale, summed[3] * grad_scale, summed[4] * grad_scale)
```

```python
import functools

import jax
import jax.numpy as jnp
import numpy as np
from jax import lax
from jax.experimental import pallas as pl
from jax.experimental.pallas import tpu as pltpu
from jax.sharding import PartitionSpec as P

NSTEP = 8
RB = 8
SR = 24
QR = 16
LANE_BIAS, LANE_MIX, LANE_MIX_BIAS, LANE_OUT = 54, 64, 96, 97
EXCH_IMAGE, EXCH_COURANT, EXCH_SPREAD, EXCH_COUNT = 16, 17, 18, 19
F32 = jnp.float32
BF16 = jnp.bfloat16


def tap_row(h, a, b, c):
    return 27 * h + 9 * a + 3 * b + c


def constants(taps, hidden):
    rep = np.zeros((RB * hidden, hidden), np.float32)
    for x in range(RB):
        rep[x * hidden : (x + 1) * hidden] = np.eye(hidden)
    wide = (RB + 2) * SR
    sel = np.zeros((3, taps, wide), np.float32)
    place = np.zeros((3, wide, 128), np.float32)
    for x in range(RB + 2):
        for b in range(3):
            for h in range(2):
                for a in range(3):
                    for c in range(3):
                        column = x * SR + h * 9 + a * 3 + c
                        sel[b, tap_row(h, a, b, c), column] = 1
                        place[b, column, tap_row(h, a, b, c)] = 1
        place[1, x * SR + 18, LANE_BIAS] = 1
    back = np.zeros((3, (RB + 2) * QR, taps), np.float32)
    for x in range(RB + 2):
        for b in range(3):
            for a in range(3):
                for c in range(3):
                    back[b, x * QR + a * 3 + c, tap_row(0, a, b, c)] = 1
    column_block = (np.arange(wide) // SR).astype(np.int32)[None]
    return (
        jnp.asarray(rep, BF16),
        jnp.asarray(sel, BF16),
        jnp.asarray(place, F32),
        jnp.asarray(back, BF16),
        jnp.asarray(column_block),
    )


def dot(a, b):
    return lax.dot_general(a, b, (((1,), (0,)), ((), ())), preferred_element_type=F32)


def dot_nt(a, b):
    return lax.dot_general(a, b, (((1,), (1,)), ((), ())), preferred_element_type=F32)


def dot_exact(a, b):
    return lax.dot_general(
        a, b, (((1,), (0,)), ((), ())), preferred_element_type=F32, precision=lax.Precision.HIGHEST
    )


def kernel(
    n,
    grad_scale,
    step_ref,
    courant,
    wave_level,
    wave_above,
    adjoint_level,
    adjoint_above,
    residual,
    wavelet,
    source_cells,
    receiver_cells,
    conv_weight,
    conv_bias,
    mix_weight,
    mix_bias,
    out_weight,
    cotangent,
    rep_ref,
    sel_ref,
    place_ref,
    back_ref,
    block_ref,
    image_out,
    first_out,
    second_out,
    input_out,
    grad_conv_out,
    grad_conv_bias_out,
    grad_mix_out,
    grad_mix_bias_out,
    grad_out_out,
    wave,
    adj,
    scaled,
    halo,
    onehot_rec,
    window,
    bf_planes,
    bf_halo,
    cot_rows,
    t_conv,
    t_mix,
    t_mix_back,
    t_taps,
    t_out,
    taps_sum,
    acc_conv,
    acc_mix,
    acc_small,
    spread_send,
    spread_halo,
    reduce_send,
    reduce_recv,
    send_sem,
    recv_sem,
    red_send_sem,
    red_recv_sem,
):
    planes, nx, ny = courant.shape
    hidden = mix_weight.shape[0]
    me = lax.axis_index("slab")
    last = n - 1
    up_id = lax.rem(me + 1, n)
    down_id = lax.rem(me + n - 1, n)
    stages = n.bit_length() - 1
    has_low = me > 0
    has_high = me < last

    barrier = pltpu.get_barrier_semaphore()

    def greet(target):
        pl.semaphore_signal(
            barrier, inc=1, device_id={"slab": target}, device_id_type=pl.DeviceIdType.MESH
        )

    @pl.when(has_low)
    def _():
        greet(down_id)

    @pl.when(has_high)
    def _():
        greet(up_id)

    def partner(stage):
        bit = 1 << stage
        return me + bit - 2 * bit * lax.rem(me // bit, 2)

    for stage in range(stages):
        greet(partner(stage))

    def remote(src, dst, ssem, rsem, target):
        return pltpu.make_async_remote_copy(
            src_ref=src,
            dst_ref=dst,
            send_sem=ssem,
            recv_sem=rsem,
            device_id={"slab": target},
            device_id_type=pl.DeviceIdType.MESH,
        )

    def pair(which, up_src, up_dst, down_src, down_dst):
        up = lambda: remote(up_src, up_dst, send_sem.at[which, 0], recv_sem.at[which, 0], up_id)
        down = lambda: remote(
            down_src, down_dst, send_sem.at[which, 1], recv_sem.at[which, 1], down_id
        )

        def start():
            @pl.when(has_high)
            def _():
                up().start()

            @pl.when(has_low)
            def _():
                down().start()

        def wait_recv():
            @pl.when(has_low)
            def _():
                up().wait_recv()

            @pl.when(has_high)
            def _():
                down().wait_recv()

        def wait_send():
            @pl.when(has_high)
            def _():
                up().wait_send()

            @pl.when(has_low)
            def _():
                down().wait_send()

        return start, wait_recv, wait_send

    def field_pair(turn, field):
        source = wave if field == 0 else scaled
        slot = turn + 1 if field == 0 else turn
        return pair(
            2 * turn + field,
            source.at[slot, planes - 1],
            halo.at[turn, field, 0],
            source.at[slot, 0],
            halo.at[turn, field, 1],
        )

    def bf_pair(channel):
        return pair(
            EXCH_IMAGE + channel,
            bf_planes.at[channel, planes - 1],
            bf_halo.at[channel, 0],
            bf_planes.at[channel, 0],
            bf_halo.at[channel, 1],
        )

    spread_pair = pair(
        EXCH_SPREAD,
        spread_send.at[0],
        spread_halo.at[0],
        spread_send.at[1],
        spread_halo.at[1],
    )

    wave[0] = wave_above[...]
    wave[1] = wave_level[...]
    adj[0] = adjoint_above[...]
    adj[1] = adjoint_level[...]
    scaled[0] = courant[...] * adjoint_level[...]
    bf_planes[1] = courant[...].astype(BF16)

    def clear(side):
        halo[:, :, side] = jnp.zeros(halo.shape[:2] + halo.shape[3:], F32)
        bf_halo[:, side] = jnp.zeros(bf_halo.shape[:1] + bf_halo.shape[2:], BF16)
        spread_halo[side] = jnp.zeros(spread_halo.shape[1:], F32)

    @pl.when(jnp.logical_not(has_low))
    def _():
        clear(0)

    @pl.when(jnp.logical_not(has_high))
    def _():
        clear(1)

    pl.semaphore_wait(
        barrier, jnp.where(has_low, 1, 0) + jnp.where(has_high, 1, 0) + stages
    )
    field_pair(0, 0)[0]()
    field_pair(0, 1)[0]()
    bf_pair(1)[0]()

    base = me * planes
    rows = planes * nx

    def row_hot(cells):
        count = cells.shape[1]
        place = (cells[0:1, :] - base) * nx + cells[1:2, :]
        return lax.broadcasted_iota(jnp.int32, (rows, count), 0) == place

    def column_hot(cells):
        count = cells.shape[1]
        hit = lax.broadcasted_iota(jnp.int32, (ny, count), 0) == cells[2:3, :]
        return jnp.where(hit, 1.0, 0.0).astype(BF16)

    onehot_rec[...] = column_hot(receiver_cells)
    source_rows = jnp.where(row_hot(source_cells), 1.0, 0.0).astype(BF16)
    source_count = dot_nt(source_rows, column_hot(source_cells))
    steps_of = wavelet.shape[1]
    pick = (
        lax.broadcasted_iota(jnp.int32, (NSTEP, steps_of), 1)
        == lax.broadcasted_iota(jnp.int32, (NSTEP, steps_of), 0) + step_ref[0]
    )
    pulses = jnp.sum(jnp.where(pick, wavelet[...], 0.0), axis=1, keepdims=True)

    row_id = lax.broadcasted_iota(jnp.int32, (nx, ny), 0)
    lane_id = lax.broadcasted_iota(jnp.int32, (nx, ny), 1)

    def from_left(v):
        return jnp.where(lane_id == 0, 0.0, pltpu.roll(v, 1, 1))

    def from_right(v):
        return jnp.where(lane_id == ny - 1, 0.0, pltpu.roll(v, ny - 1, 1))

    def lap_plane(v):
        total = jnp.where(row_id == nx - 1, 0.0, pltpu.roll(v, nx - 1, 0))
        total += jnp.where(row_id == 0, 0.0, pltpu.roll(v, 1, 0))
        return total + from_right(v) + from_left(v) - 6.0 * v

    def laplace(ref, slot, turn, field):
        volume = [ref[slot, p] for p in range(planes)]
        inner = [lap_plane(v) for v in volume]
        field_pair(turn, field)[1]()
        volume = [halo[turn, field, 0]] + volume + [halo[turn, field, 1]]
        return [inner[p] + volume[p] + volume[p + 2] for p in range(planes)]

    def records_of(level):
        data = residual[pl.ds(level - 1, 1), :]
        spread = jnp.where(row_hot(receiver_cells), data, 0.0)
        top = spread.astype(BF16)
        rest = spread - top.astype(F32)
        middle = rest.astype(BF16)
        low = (rest - middle.astype(F32)).astype(BF16)
        columns = onehot_rec[...]
        return dot_nt(top, columns) + (dot_nt(middle, columns) + dot_nt(low, columns))

    image_out[...] = jnp.zeros(image_out.shape, F32)

    def turn_of(turn):
        level = NSTEP - turn
        records = records_of(level)
        pulse = pulses[level - 1 : level, :]
        lap_wave = laplace(wave, turn + 1, turn, 0)
        for p in range(planes):
            cell_rows = slice(p * nx, (p + 1) * nx)
            image_out[p] += adj[turn + 1, p] * lap_wave[p]
            if turn + 1 < NSTEP:
                wave[turn + 2, p] = (
                    2.0 * wave[turn + 1, p]
                    - wave[turn, p]
                    + courant[p] * lap_wave[p]
                    + source_count[cell_rows] * pulse
                )
        if turn + 1 < NSTEP:
            field_pair(turn + 1, 0)[0]()
        lap_adj = laplace(scaled, turn, turn, 1)
        for p in range(planes):
            cell_rows = slice(p * nx, (p + 1) * nx)
            lower = 2.0 * adj[turn + 1, p] - adj[turn, p] + lap_adj[p] + records[cell_rows]
            if turn + 1 < NSTEP:
                adj[turn + 2, p] = lower
                scaled[turn + 1, p] = courant[p] * lower
            else:
                first_out[p] = lower
        if turn + 1 < NSTEP:
            field_pair(turn + 1, 1)[0]()

    def put_plane(channel, plane, values):
        shifted = (from_left(values), values, from_right(values))
        for z in range(planes):
            a = plane - z
            if 0 <= a < 3:
                for c in range(3):
                    at = SR + channel * 9 + a * 3 + c
                    for half in range(ny // 128):
                        part = shifted[c][:, half * 128 : (half + 1) * 128]
                        window[z, half, pl.ds(at, nx, stride=SR), :] = part

    window[...] = jnp.zeros(window.shape, F32)
    for z in range(planes):
        for half in range(ny // 128):
            window[z, half, pl.ds(SR + 18, nx, stride=SR), :] = jnp.ones((nx, 128), F32)
    for p in range(planes):
        put_plane(1, p + 1, bf_planes[1, p].astype(F32))
    cot_rows[...] = cotangent[...].astype(F32)

    wide = (RB + 2) * SR
    tall = RB * hidden
    rep = rep_ref[...]
    tiled = dot_nt(rep, conv_weight[...]).astype(BF16)
    row_block = lax.broadcasted_iota(jnp.int32, (tall, wide), 0) // hidden
    band = [row_block + b == block_ref[...] for b in range(3)]
    conv_banded = jnp.zeros((tall, wide), F32)
    for b in range(3):
        conv_banded += jnp.where(band[b], dot(tiled, sel_ref[b]), 0.0)
    t_conv[...] = conv_banded.astype(BF16)
    diagonal = (
        lax.broadcasted_iota(jnp.int32, (tall, tall), 0) // hidden
        == lax.broadcasted_iota(jnp.int32, (tall, tall), 1) // hidden
    )
    mixed = dot_nt(dot_nt(rep, mix_weight[...]).astype(BF16), rep)
    t_mix[...] = jnp.where(diagonal, mixed, 0.0).astype(BF16)
    mixed_back = dot_nt(dot(rep, mix_weight[...]).astype(BF16), rep)
    t_mix_back[...] = jnp.where(diagonal, mixed_back, 0.0).astype(BF16)
    back_rows = (RB + 2) * QR
    back_row = lax.broadcasted_iota(jnp.int32, (back_rows, tall), 0) // QR
    back_column = lax.broadcasted_iota(jnp.int32, (back_rows, tall), 1) // hidden
    taps_banded = jnp.zeros((back_rows, tall), F32)
    for b in range(3):
        part = dot_nt(dot(back_ref[b], conv_weight[...]).astype(BF16), rep)
        taps_banded += jnp.where(back_column + b == back_row, part, 0.0)
    t_taps[...] = taps_banded.astype(BF16)
    rep_wide = rep.astype(F32)

    def column_of(vector):
        return jnp.sum(rep_wide * vector[...].astype(F32), axis=1, keepdims=True)

    bias_one = column_of(conv_bias)
    bias_two = column_of(mix_bias)
    out_diagonal = (
        lax.broadcasted_iota(jnp.int32, (tall, RB), 0) // hidden
        == lax.broadcasted_iota(jnp.int32, (tall, RB), 1)
    )
    t_out[...] = jnp.where(out_diagonal, column_of(out_weight), 0.0).astype(BF16)
    taps_sum[...] = jnp.zeros(taps_sum.shape, F32)
    acc_conv[...] = jnp.zeros(acc_conv.shape, F32)
    acc_mix[...] = jnp.zeros(acc_mix.shape, F32)
    acc_small[...] = jnp.zeros(acc_small.shape, F32)

    for turn in range(NSTEP):
        turn_of(turn)

    for p in range(planes):
        bf_planes[0, p] = image_out[p].astype(BF16)
    bf_pair(0)[0]()
    second_out[...] = adj[NSTEP]
    for p in range(planes):
        put_plane(0, p + 1, bf_planes[0, p].astype(F32))
    bf_pair(1)[1]()
    put_plane(1, 0, bf_halo[1, 0].astype(F32))
    put_plane(1, planes + 1, bf_halo[1, 1].astype(F32))
    bf_pair(0)[1]()
    put_plane(0, 0, bf_halo[0, 0].astype(F32))
    put_plane(0, planes + 1, bf_halo[0, 1].astype(F32))

    blocks = nx // RB

    def block_of(z, x):
        where = pl.ds(pl.multiple_of(x * (RB * SR), 8), wide)
        halves = [window[z, half, where, :] for half in range(ny // 128)]
        piece = jnp.concatenate(halves, axis=1).astype(BF16)
        cot = cot_rows[z, pl.ds(pl.multiple_of(x * RB, RB), RB), :].astype(BF16)
        pre_one = dot(t_conv[...], piece) + bias_one
        sig_one = 0.5 * jnp.tanh(0.5 * pre_one) + 0.5
        act_one = (pre_one * sig_one).astype(BF16)
        slope_one = sig_one * (1.0 + pre_one * (1.0 - sig_one))
        pre_two = dot(t_mix[...], act_one) + bias_two
        sig_two = 0.5 * jnp.tanh(0.5 * pre_two) + 0.5
        act_two = (pre_two * sig_two).astype(BF16)
        slope_two = sig_two * (1.0 + pre_two * (1.0 - sig_two))
        grad_two = (dot(t_out[...], cot) * slope_two).astype(BF16)
        grad_one = (dot(t_mix_back[...], grad_two) * slope_one).astype(BF16)
        acc_conv[...] += dot_nt(grad_one, piece)
        acc_mix[...] += dot_nt(grad_two, act_one)
        acc_small[0] += dot_nt(act_two, cot)
        acc_small[1] += dot_nt(grad_two, jnp.ones((RB, ny), BF16))
        where = pl.ds(pl.multiple_of(x * (RB * QR), 8), back_rows)
        spread = dot(t_taps[...], grad_one)
        for half in range(ny // 128):
            taps_sum[z, half, where, :] += spread[:, half * 128 : (half + 1) * 128]

    def block_loop(index, carried):
        block_of(index // blocks, lax.rem(index, blocks))
        return carried

    lax.fori_loop(0, planes * blocks, block_loop, 0)

    def fold(values):
        total = values[0:hidden]
        for x in range(1, RB):
            total = total + values[x * hidden : (x + 1) * hidden]
        return total

    conv_sum = acc_conv[...]
    packed = jnp.zeros((hidden, 128), F32)
    for b in range(3):
        packed += dot_exact(fold(jnp.where(band[b], conv_sum, 0.0)), place_ref[b])
    mix_at = lax.broadcasted_iota(jnp.int32, (tall, 128), 1) - LANE_MIX
    mix_place = mix_at == lax.rem(lax.broadcasted_iota(jnp.int32, (tall, 128), 0), hidden)
    packed += dot_exact(
        fold(jnp.where(diagonal, acc_mix[...], 0.0)), jnp.where(mix_place, 1.0, 0.0)
    )
    out_sum = fold(
        jnp.sum(jnp.where(out_diagonal, acc_small[0], 0.0), axis=1, keepdims=True)
    )
    mix_bias_sum = fold(acc_small[1][:, 0:1])
    packed_lane = lax.broadcasted_iota(jnp.int32, (hidden, 128), 1)
    packed = jnp.where(packed_lane == LANE_OUT, out_sum, packed)
    packed = jnp.where(packed_lane == LANE_MIX_BIAS, mix_bias_sum, packed)

    def reduce_copy(stage):
        return remote(
            reduce_send.at[stage],
            reduce_recv.at[stage],
            red_send_sem.at[stage],
            red_recv_sem.at[stage],
            partner(stage),
        )

    reduce_send[0] = packed
    if stages:
        reduce_copy(0).start()

    def spread_of(z, a):
        base_row = QR + a * 3


        def take(c):
            where = pl.ds(base_row + c, nx, stride=QR)
            return jnp.concatenate(
                [taps_sum[z, half, where, :] for half in range(ny // 128)], axis=1
            )

        return from_right(take(0)) + take(1) + from_left(take(2))

    spread_send[0] = spread_of(planes - 1, 2)
    spread_send[1] = spread_of(0, 0)
    spread_pair[0]()

    def finish_stage(stage):
        reduce_copy(stage).wait_recv()
        reduce_send[stage + 1] = reduce_send[stage] + reduce_recv[stage]
        if stage + 1 < stages:
            reduce_copy(stage + 1).start()

    if stages:
        finish_stage(0)
    for p in range(planes):
        total = spread_of(p, 1)
        if p > 0:
            total = total + spread_of(p - 1, 2)
        if p + 1 < planes:
            total = total + spread_of(p + 1, 0)
        input_out[p] = total
    for stage in range(1, stages):
        finish_stage(stage)
    spread_pair[1]()
    input_out[0] += spread_halo[0]
    input_out[planes - 1] += spread_halo[1]

    summed = reduce_send[stages] * grad_scale
    eye = (
        lax.broadcasted_iota(jnp.int32, (128, 128), 0)
        == lax.broadcasted_iota(jnp.int32, (128, 128), 1)
    )
    turned = lax.dot_general(
        jnp.where(eye, 1.0, 0.0),
        summed,
        (((1,), (1,)), ((), ())),
        preferred_element_type=F32,
        precision=lax.Precision.HIGHEST,
    )
    taps = conv_weight.shape[0]
    grad_conv_out[...] = turned[0:taps]
    grad_conv_bias_out[...] = turned[LANE_BIAS : LANE_BIAS + 1]
    grad_mix_out[...] = turned[LANE_MIX : LANE_MIX + hidden]
    grad_mix_bias_out[...] = turned[LANE_MIX_BIAS : LANE_MIX_BIAS + 1]
    grad_out_out[...] = turned[LANE_OUT : LANE_OUT + 1]

    for turn in range(NSTEP):
        for field in range(2):
            field_pair(turn, field)[2]()
    for channel in range(2):
        bf_pair(channel)[2]()
    spread_pair[2]()
    for stage in range(stages):
        reduce_copy(stage).wait_send()


def on_device(
    courant,
    wave_level,
    wave_above,
    adjoint_level,
    adjoint_above,
    residual_data,
    wavelet,
    checkpoint_step,
    source_cells,
    receiver_cells,
    conv_weight,
    conv_bias,
    mix_weight,
    mix_bias,
    out_weight,
    update_cotangent,
):
    n = lax.axis_size("slab")
    planes, nx, ny = courant.shape
    taps, hidden = conv_weight.shape
    receivers = receiver_cells.shape[1]
    stages = n.bit_length() - 1
    grad_scale = float(n * planes * nx * ny) ** (-0.5)
    grid = (planes, nx, ny)
    tall = RB * hidden
    wide = (RB + 2) * SR
    vmem = pl.BlockSpec(memory_space=pltpu.VMEM)
    smem = pl.BlockSpec(memory_space=pltpu.SMEM)
    consts = constants(taps, hidden)
    outs = pl.pallas_call(
        functools.partial(kernel, n, grad_scale),
        out_shape=(
            jax.ShapeDtypeStruct(grid, F32),
            jax.ShapeDtypeStruct(grid, F32),
            jax.ShapeDtypeStruct(grid, F32),
            jax.ShapeDtypeStruct(grid, F32),
            jax.ShapeDtypeStruct((taps, hidden), F32),
            jax.ShapeDtypeStruct((1, hidden), F32),
            jax.ShapeDtypeStruct((hidden, hidden), F32),
            jax.ShapeDtypeStruct((1, hidden), F32),
            jax.ShapeDtypeStruct((1, hidden), F32),
        ),
        in_specs=[smem] + [vmem] * (15 + len(consts)),
        out_specs=(vmem,) * 9,
        scratch_shapes=[
            pltpu.VMEM((NSTEP + 1,) + grid, F32),
            pltpu.VMEM((NSTEP + 1,) + grid, F32),
            pltpu.VMEM((NSTEP,) + grid, F32),
            pltpu.VMEM((NSTEP, 2, 2, nx, ny), F32),
            pltpu.VMEM((ny, receivers), BF16),
            pltpu.VMEM((planes, ny // 128, (nx + 2) * SR, 128), F32),
            pltpu.VMEM((2,) + grid, BF16),
            pltpu.VMEM((2, 2, nx, ny), BF16),
            pltpu.VMEM(grid, F32),
            pltpu.VMEM((tall, wide), BF16),
            pltpu.VMEM((tall, tall), BF16),
            pltpu.VMEM((tall, tall), BF16),
            pltpu.VMEM(((RB + 2) * QR, tall), BF16),
            pltpu.VMEM((tall, RB), BF16),
            pltpu.VMEM((planes, ny // 128, (nx + 2) * QR, 128), F32),
            pltpu.VMEM((tall, wide), F32),
            pltpu.VMEM((tall, tall), F32),
            pltpu.VMEM((2, tall, RB), F32),
            pltpu.VMEM((2, nx, ny), F32),
            pltpu.VMEM((2, nx, ny), F32),
            pltpu.VMEM((stages + 1, hidden, 128), F32),
            pltpu.VMEM((max(stages, 1), hidden, 128), F32),
            pltpu.SemaphoreType.DMA((EXCH_COUNT, 2)),
            pltpu.SemaphoreType.DMA((EXCH_COUNT, 2)),
            pltpu.SemaphoreType.DMA((max(stages, 1),)),
            pltpu.SemaphoreType.DMA((max(stages, 1),)),
        ],
        compiler_params=pltpu.CompilerParams(
            collective_id=0, has_side_effects=True, vmem_limit_bytes=48 * 1024 * 1024
        ),
    )(
        checkpoint_step,
        courant,
        wave_level,
        wave_above,
        adjoint_level,
        adjoint_above,
        residual_data,
        wavelet[None],
        source_cells,
        receiver_cells,
        conv_weight,
        conv_bias[None],
        mix_weight,
        mix_bias[None],
        out_weight[None],
        update_cotangent,
        *consts,
    )
    return outs[:5] + (outs[5][0], outs[6], outs[7][0], outs[8][0])


def solution(mesh):
    slabs = P(("grp", "slab"), None, None)
    return jax.shard_map(
        on_device,
        mesh=mesh,
        in_specs=(slabs,) * 5
        + (P(None, "grp"), P("grp"), P("grp"), P(None, "grp"), P(None, "grp"))
        + (P(),) * 5
        + (slabs,),
        out_specs=(slabs,) * 4 + (P("grp", None), P("grp"), P("grp", None), P("grp"), P("grp")),
        check_vma=False,
    )
```

```python
import functools

import jax
import jax.numpy as jnp
import numpy as np
from jax import lax
from jax.experimental import pallas as pl
from jax.experimental.pallas import tpu as pltpu
from jax.sharding import PartitionSpec as P

NSTEP = 8
VMEM_LIMIT = int(63.5 * 1024 * 1024)
RB = 8
SR = 24
QR = 16
LANE_BIAS, LANE_MIX, LANE_MIX_BIAS, LANE_OUT = 54, 64, 96, 97
EXCH_IMAGE, EXCH_COURANT, EXCH_SPREAD, EXCH_COUNT = 16, 17, 18, 19
F32 = jnp.float32
BF16 = jnp.bfloat16


def tap_row(h, a, b, c):
    return 27 * h + 9 * a + 3 * b + c


def constants(taps, hidden):
    rep = np.zeros((RB * hidden, hidden), np.float32)
    for x in range(RB):
        rep[x * hidden : (x + 1) * hidden] = np.eye(hidden)
    wide = (RB + 2) * SR
    sel = np.zeros((3, taps, wide), np.float32)
    place = np.zeros((3, wide, 128), np.float32)
    for x in range(RB + 2):
        for b in range(3):
            for h in range(2):
                for a in range(3):
                    for c in range(3):
                        column = x * SR + h * 9 + a * 3 + c
                        sel[b, tap_row(h, a, b, c), column] = 1
                        place[b, column, tap_row(h, a, b, c)] = 1
        place[1, x * SR + 18, LANE_BIAS] = 1
    back = np.zeros((3, (RB + 2) * QR, taps), np.float32)
    for x in range(RB + 2):
        for b in range(3):
            for a in range(3):
                for c in range(3):
                    back[b, x * QR + a * 3 + c, tap_row(0, a, b, c)] = 1
    column_block = (np.arange(wide) // SR).astype(np.int32)[None]
    return (
        jnp.asarray(rep, BF16),
        jnp.asarray(sel, BF16),
        jnp.asarray(place, F32),
        jnp.asarray(back, BF16),
        jnp.asarray(column_block),
    )


def dot(a, b):
    return lax.dot_general(a, b, (((1,), (0,)), ((), ())), preferred_element_type=F32)


def dot_nt(a, b):
    return lax.dot_general(a, b, (((1,), (1,)), ((), ())), preferred_element_type=F32)


def dot_exact(a, b):
    return lax.dot_general(
        a, b, (((1,), (0,)), ((), ())), preferred_element_type=F32, precision=lax.Precision.HIGHEST
    )


def kernel(
    n,
    grad_scale,
    step_hbm,
    courant_hbm,
    wave_level_hbm,
    wave_above_hbm,
    adjoint_level_hbm,
    adjoint_above_hbm,
    residual_hbm,
    wavelet_hbm,
    source_cells_hbm,
    receiver_cells_hbm,
    conv_weight_hbm,
    conv_bias_hbm,
    mix_weight_hbm,
    mix_bias_hbm,
    out_weight_hbm,
    cotangent_hbm,
    rep_ref_hbm,
    sel_ref_hbm,
    place_ref_hbm,
    back_ref_hbm,
    block_ref_hbm,
    image_out_hbm,
    first_out_hbm,
    second_out_hbm,
    input_out_hbm,
    grad_conv_out_hbm,
    grad_conv_bias_out_hbm,
    grad_mix_out_hbm,
    grad_mix_bias_out_hbm,
    grad_out_out_hbm,
    wave,
    adj,
    scaled,
    halo,
    onehot_rec,
    window,
    bf_planes,
    bf_halo,
    cot_rows,
    t_conv,
    t_mix,
    t_mix_back,
    t_taps,
    t_out,
    taps_sum,
    acc_conv,
    acc_mix,
    acc_small,
    spread_send,
    spread_halo,
    reduce_send,
    reduce_recv,
    send_sem,
    recv_sem,
    red_send_sem,
    red_recv_sem,
    in_sem,
    out_sem,
    image_out,
    first_out,
    input_out,
    grad_conv_out,
    grad_conv_bias_out,
    grad_mix_out,
    grad_mix_bias_out,
    grad_out_out,
    step_ref,
    courant,
    residual,
    wavelet,
    source_cells,
    receiver_cells,
    conv_weight,
    conv_bias,
    mix_weight,
    mix_bias,
    out_weight,
    cotangent,
    rep_ref,
    sel_ref,
    place_ref,
    back_ref,
    block_ref,
):
    planes, nx, ny = courant.shape
    hidden = mix_weight.shape[0]
    me = lax.axis_index("slab")
    last = n - 1
    up_id = lax.rem(me + 1, n)
    down_id = lax.rem(me + n - 1, n)
    stages = n.bit_length() - 1
    has_low = me > 0
    has_high = me < last

    barrier = pltpu.get_barrier_semaphore()

    def greet(target):
        pl.semaphore_signal(
            barrier, inc=1, device_id={"slab": target}, device_id_type=pl.DeviceIdType.MESH
        )

    @pl.when(has_low)
    def _():
        greet(down_id)

    @pl.when(has_high)
    def _():
        greet(up_id)

    def partner(stage):
        bit = 1 << stage
        return me + bit - 2 * bit * lax.rem(me // bit, 2)

    for stage in range(stages):
        greet(partner(stage))

    loads = {
        "courant": (courant_hbm, courant),
        "adjoint_level": (adjoint_level_hbm, adj.at[1]),
        "wave_level": (wave_level_hbm, wave.at[1]),
        "receiver_cells": (receiver_cells_hbm, receiver_cells),
        "residual": (residual_hbm, residual),
        "source_cells": (source_cells_hbm, source_cells),
        "wavelet": (wavelet_hbm, wavelet),
        "step": (step_hbm, step_ref),
        "wave_above": (wave_above_hbm, wave.at[0]),
        "adjoint_above": (adjoint_above_hbm, adj.at[0]),
        "cotangent": (cotangent_hbm, cotangent),
        "rep_ref": (rep_ref_hbm, rep_ref),
        "conv_weight": (conv_weight_hbm, conv_weight),
        "sel_ref": (sel_ref_hbm, sel_ref),
        "block_ref": (block_ref_hbm, block_ref),
        "mix_weight": (mix_weight_hbm, mix_weight),
        "back_ref": (back_ref_hbm, back_ref),
        "conv_bias": (conv_bias_hbm, conv_bias),
        "mix_bias": (mix_bias_hbm, mix_bias),
        "out_weight": (out_weight_hbm, out_weight),
        "place_ref": (place_ref_hbm, place_ref),
    }
    loads = {
        name: pltpu.make_async_copy(src, dst, in_sem.at[index])
        for index, (name, (src, dst)) in enumerate(loads.items())
    }
    for copy in loads.values():
        copy.start()

    def loaded(*wanted):
        for name in wanted:
            loads.pop(name).wait()

    def remote(src, dst, ssem, rsem, target):
        return pltpu.make_async_remote_copy(
            src_ref=src,
            dst_ref=dst,
            send_sem=ssem,
            recv_sem=rsem,
            device_id={"slab": target},
            device_id_type=pl.DeviceIdType.MESH,
        )

    def pair(which, up_src, up_dst, down_src, down_dst):
        up = lambda: remote(up_src, up_dst, send_sem.at[which, 0], recv_sem.at[which, 0], up_id)
        down = lambda: remote(
            down_src, down_dst, send_sem.at[which, 1], recv_sem.at[which, 1], down_id
        )

        def start():
            @pl.when(has_high)
            def _():
                up().start()

            @pl.when(has_low)
            def _():
                down().start()

        def wait_recv():
            @pl.when(has_low)
            def _():
                up().wait_recv()

            @pl.when(has_high)
            def _():
                down().wait_recv()

        def wait_send():
            @pl.when(has_high)
            def _():
                up().wait_send()

            @pl.when(has_low)
            def _():
                down().wait_send()

        return start, wait_recv, wait_send

    def field_pair(turn, field):
        source = wave if field == 0 else scaled
        slot = turn + 1 if field == 0 else turn
        return pair(
            2 * turn + field,
            source.at[slot, planes - 1],
            halo.at[turn, field, 0],
            source.at[slot, 0],
            halo.at[turn, field, 1],
        )

    def bf_pair(channel):
        return pair(
            EXCH_IMAGE + channel,
            bf_planes.at[channel, planes - 1],
            bf_halo.at[channel, 0],
            bf_planes.at[channel, 0],
            bf_halo.at[channel, 1],
        )

    spread_pair = pair(
        EXCH_SPREAD,
        spread_send.at[0],
        spread_halo.at[0],
        spread_send.at[1],
        spread_halo.at[1],
    )

    loaded("courant", "adjoint_level", "wave_level")
    scaled[0] = courant[...] * adj[1]
    bf_planes[1] = courant[...].astype(BF16)

    def clear(side):
        halo[:, :, side] = jnp.zeros(halo.shape[:2] + halo.shape[3:], F32)
        bf_halo[:, side] = jnp.zeros(bf_halo.shape[:1] + bf_halo.shape[2:], BF16)
        spread_halo[side] = jnp.zeros(spread_halo.shape[1:], F32)

    @pl.when(jnp.logical_not(has_low))
    def _():
        clear(0)

    @pl.when(jnp.logical_not(has_high))
    def _():
        clear(1)

    pl.semaphore_wait(
        barrier, jnp.where(has_low, 1, 0) + jnp.where(has_high, 1, 0) + stages
    )
    field_pair(0, 0)[0]()
    field_pair(0, 1)[0]()
    bf_pair(1)[0]()

    base = me * planes
    rows = planes * nx

    def row_hot(cells):
        count = cells.shape[1]
        place = (cells[0:1, :] - base) * nx + cells[1:2, :]
        return lax.broadcasted_iota(jnp.int32, (rows, count), 0) == place

    def column_hot(cells):
        count = cells.shape[1]
        hit = lax.broadcasted_iota(jnp.int32, (ny, count), 0) == cells[2:3, :]
        return jnp.where(hit, 1.0, 0.0).astype(BF16)

    loaded("receiver_cells", "residual", "source_cells", "wavelet", "step")
    onehot_rec[...] = column_hot(receiver_cells)
    source_rows = jnp.where(row_hot(source_cells), 1.0, 0.0).astype(BF16)
    source_count = dot_nt(source_rows, column_hot(source_cells))
    steps_of = wavelet.shape[1]
    pick = (
        lax.broadcasted_iota(jnp.int32, (NSTEP, steps_of), 1)
        == lax.broadcasted_iota(jnp.int32, (NSTEP, steps_of), 0) + step_ref[0]
    )
    pulses = jnp.sum(jnp.where(pick, wavelet[...], 0.0), axis=1, keepdims=True)

    row_id = lax.broadcasted_iota(jnp.int32, (nx, ny), 0)
    lane_id = lax.broadcasted_iota(jnp.int32, (nx, ny), 1)

    def from_left(v):
        return jnp.where(lane_id == 0, 0.0, pltpu.roll(v, 1, 1))

    def from_right(v):
        return jnp.where(lane_id == ny - 1, 0.0, pltpu.roll(v, ny - 1, 1))

    def lap_plane(v):
        total = jnp.where(row_id == nx - 1, 0.0, pltpu.roll(v, nx - 1, 0))
        total += jnp.where(row_id == 0, 0.0, pltpu.roll(v, 1, 0))
        return total + from_right(v) + from_left(v) - 6.0 * v

    def laplace(ref, slot, turn, field):
        volume = [ref[slot, p] for p in range(planes)]
        inner = [lap_plane(v) for v in volume]
        field_pair(turn, field)[1]()
        volume = [halo[turn, field, 0]] + volume + [halo[turn, field, 1]]
        return [inner[p] + volume[p] + volume[p + 2] for p in range(planes)]

    def records_of(level):
        data = residual[pl.ds(level - 1, 1), :]
        spread = jnp.where(row_hot(receiver_cells), data, 0.0)
        top = spread.astype(BF16)
        rest = spread - top.astype(F32)
        middle = rest.astype(BF16)
        low = (rest - middle.astype(F32)).astype(BF16)
        columns = onehot_rec[...]
        return dot_nt(top, columns) + (dot_nt(middle, columns) + dot_nt(low, columns))

    image_out[...] = jnp.zeros(image_out.shape, F32)
    stores = []

    def store(index, src, dst):
        copy = pltpu.make_async_copy(src, dst, out_sem.at[index])
        copy.start()
        stores.append(copy)

    def turn_of(turn):
        level = NSTEP - turn
        records = records_of(level)
        pulse = pulses[level - 1 : level, :]
        lap_wave = laplace(wave, turn + 1, turn, 0)
        for p in range(planes):
            cell_rows = slice(p * nx, (p + 1) * nx)
            image_out[p] += adj[turn + 1, p] * lap_wave[p]
            if turn + 1 < NSTEP:
                wave[turn + 2, p] = (
                    2.0 * wave[turn + 1, p]
                    - wave[turn, p]
                    + courant[p] * lap_wave[p]
                    + source_count[cell_rows] * pulse
                )
        if turn + 1 < NSTEP:
            field_pair(turn + 1, 0)[0]()
        lap_adj = laplace(scaled, turn, turn, 1)
        for p in range(planes):
            cell_rows = slice(p * nx, (p + 1) * nx)
            lower = 2.0 * adj[turn + 1, p] - adj[turn, p] + lap_adj[p] + records[cell_rows]
            if turn + 1 < NSTEP:
                adj[turn + 2, p] = lower
                scaled[turn + 1, p] = courant[p] * lower
            else:
                first_out[p] = lower
        if turn + 1 < NSTEP:
            field_pair(turn + 1, 1)[0]()

    def put_plane(channel, plane, values):
        shifted = (from_left(values), values, from_right(values))
        for z in range(planes):
            a = plane - z
            if 0 <= a < 3:
                for c in range(3):
                    at = SR + channel * 9 + a * 3 + c
                    for half in range(ny // 128):
                        part = shifted[c][:, half * 128 : (half + 1) * 128]
                        window[z, half, pl.ds(at, nx, stride=SR), :] = part

    window[...] = jnp.zeros(window.shape, F32)
    for z in range(planes):
        for half in range(ny // 128):
            window[z, half, pl.ds(SR + 18, nx, stride=SR), :] = jnp.ones((nx, 128), F32)
    for p in range(planes):
        put_plane(1, p + 1, bf_planes[1, p].astype(F32))
    loaded(*tuple(loads))
    cot_rows[...] = cotangent[...].astype(F32)

    wide = (RB + 2) * SR
    tall = RB * hidden
    rep = rep_ref[...]
    tiled = dot(rep, conv_weight[...]).astype(BF16)
    row_block = lax.broadcasted_iota(jnp.int32, (tall, wide), 0) // hidden
    band = [row_block + b == block_ref[...] for b in range(3)]
    conv_banded = jnp.zeros((tall, wide), F32)
    for b in range(3):
        conv_banded += jnp.where(band[b], dot(tiled, sel_ref[b]), 0.0)
    t_conv[...] = conv_banded.astype(BF16)
    diagonal = (
        lax.broadcasted_iota(jnp.int32, (tall, tall), 0) // hidden
        == lax.broadcasted_iota(jnp.int32, (tall, tall), 1) // hidden
    )
    mixed = dot_nt(dot_nt(rep, mix_weight[...]).astype(BF16), rep)
    t_mix[...] = jnp.where(diagonal, mixed, 0.0).astype(BF16)
    mixed_back = dot_nt(dot(rep, mix_weight[...]).astype(BF16), rep)
    t_mix_back[...] = jnp.where(diagonal, mixed_back, 0.0).astype(BF16)
    back_rows = (RB + 2) * QR
    back_row = lax.broadcasted_iota(jnp.int32, (back_rows, tall), 0) // QR
    back_column = lax.broadcasted_iota(jnp.int32, (back_rows, tall), 1) // hidden
    taps_banded = jnp.zeros((back_rows, tall), F32)
    for b in range(3):
        part = dot_nt(dot_nt(back_ref[b], conv_weight[...]).astype(BF16), rep)
        taps_banded += jnp.where(back_column + b == back_row, part, 0.0)
    t_taps[...] = taps_banded.astype(BF16)
    rep_wide = rep.astype(F32)

    def column_of(vector):
        return jnp.sum(rep_wide * vector[...].astype(F32), axis=1, keepdims=True)

    bias_one = column_of(conv_bias)
    bias_two = column_of(mix_bias)
    out_diagonal = (
        lax.broadcasted_iota(jnp.int32, (tall, RB), 0) // hidden
        == lax.broadcasted_iota(jnp.int32, (tall, RB), 1)
    )
    t_out[...] = jnp.where(out_diagonal, column_of(out_weight), 0.0).astype(BF16)
    taps_sum[...] = jnp.zeros(taps_sum.shape, F32)
    acc_conv[...] = jnp.zeros(acc_conv.shape, F32)
    acc_mix[...] = jnp.zeros(acc_mix.shape, F32)
    acc_small[...] = jnp.zeros(acc_small.shape, F32)

    for turn in range(NSTEP):
        turn_of(turn)

    for p in range(planes):
        bf_planes[0, p] = image_out[p].astype(BF16)
    bf_pair(0)[0]()
    store(0, image_out, image_out_hbm)
    store(1, first_out, first_out_hbm)
    store(2, adj.at[NSTEP], second_out_hbm)
    for p in range(planes):
        put_plane(0, p + 1, bf_planes[0, p].astype(F32))
    bf_pair(1)[1]()
    put_plane(1, 0, bf_halo[1, 0].astype(F32))
    put_plane(1, planes + 1, bf_halo[1, 1].astype(F32))
    bf_pair(0)[1]()
    put_plane(0, 0, bf_halo[0, 0].astype(F32))
    put_plane(0, planes + 1, bf_halo[0, 1].astype(F32))

    blocks = nx // RB

    def block_of(z, x):
        where = pl.ds(pl.multiple_of(x * (RB * SR), 8), wide)
        halves = [window[z, half, where, :] for half in range(ny // 128)]
        piece = jnp.concatenate(halves, axis=1).astype(BF16)
        cot = cot_rows[z, pl.ds(pl.multiple_of(x * RB, RB), RB), :].astype(BF16)
        pre_one = dot(t_conv[...], piece) + bias_one
        sig_one = 0.5 * jnp.tanh(0.5 * pre_one) + 0.5
        act_one = (pre_one * sig_one).astype(BF16)
        slope_one = sig_one * (1.0 + pre_one * (1.0 - sig_one))
        pre_two = dot(t_mix[...], act_one) + bias_two
        sig_two = 0.5 * jnp.tanh(0.5 * pre_two) + 0.5
        act_two = (pre_two * sig_two).astype(BF16)
        slope_two = sig_two * (1.0 + pre_two * (1.0 - sig_two))
        grad_two = (dot(t_out[...], cot) * slope_two).astype(BF16)
        grad_one = (dot(t_mix_back[...], grad_two) * slope_one).astype(BF16)
        acc_conv[...] += dot_nt(grad_one, piece)
        acc_mix[...] += dot_nt(grad_two, act_one)
        acc_small[0] += dot_nt(act_two, cot)
        acc_small[1] += dot_nt(grad_two, jnp.ones((RB, ny), BF16))
        where = pl.ds(pl.multiple_of(x * (RB * QR), 8), back_rows)
        spread = dot(t_taps[...], grad_one)
        for half in range(ny // 128):
            taps_sum[z, half, where, :] += spread[:, half * 128 : (half + 1) * 128]

    def block_loop(index, carried):
        block_of(index // blocks, lax.rem(index, blocks))
        return carried

    lax.fori_loop(0, planes * blocks, block_loop, 0)

    def fold(values):
        total = values[0:hidden]
        for x in range(1, RB):
            total = total + values[x * hidden : (x + 1) * hidden]
        return total

    conv_sum = acc_conv[...]
    packed = jnp.zeros((hidden, 128), F32)
    for b in range(3):
        packed += dot_exact(fold(jnp.where(band[b], conv_sum, 0.0)), place_ref[b])
    mix_at = lax.broadcasted_iota(jnp.int32, (tall, 128), 1) - LANE_MIX
    mix_place = mix_at == lax.rem(lax.broadcasted_iota(jnp.int32, (tall, 128), 0), hidden)
    packed += dot_exact(
        fold(jnp.where(diagonal, acc_mix[...], 0.0)), jnp.where(mix_place, 1.0, 0.0)
    )
    out_sum = fold(
        jnp.sum(jnp.where(out_diagonal, acc_small[0], 0.0), axis=1, keepdims=True)
    )
    mix_bias_sum = fold(acc_small[1][:, 0:1])
    packed_lane = lax.broadcasted_iota(jnp.int32, (hidden, 128), 1)
    packed = jnp.where(packed_lane == LANE_OUT, out_sum, packed)
    packed = jnp.where(packed_lane == LANE_MIX_BIAS, mix_bias_sum, packed)

    def reduce_copy(stage):
        return remote(
            reduce_send.at[stage],
            reduce_recv.at[stage],
            red_send_sem.at[stage],
            red_recv_sem.at[stage],
            partner(stage),
        )

    reduce_send[0] = packed
    if stages:
        reduce_copy(0).start()

    def spread_of(z, a):
        base_row = QR + a * 3


        def take(c):
            where = pl.ds(base_row + c, nx, stride=QR)
            return jnp.concatenate(
                [taps_sum[z, half, where, :] for half in range(ny // 128)], axis=1
            )

        return from_right(take(0)) + take(1) + from_left(take(2))

    spread_send[0] = spread_of(planes - 1, 2)
    spread_send[1] = spread_of(0, 0)
    spread_pair[0]()

    def finish_stage(stage):
        reduce_copy(stage).wait_recv()
        reduce_send[stage + 1] = reduce_send[stage] + reduce_recv[stage]
        if stage + 1 < stages:
            reduce_copy(stage + 1).start()

    if stages:
        finish_stage(0)
    for p in range(planes):
        total = spread_of(p, 1)
        if p > 0:
            total = total + spread_of(p - 1, 2)
        if p + 1 < planes:
            total = total + spread_of(p + 1, 0)
        input_out[p] = total
    for stage in range(1, stages):
        finish_stage(stage)
    spread_pair[1]()
    input_out[0] += spread_halo[0]
    input_out[planes - 1] += spread_halo[1]
    store(3, input_out, input_out_hbm)

    summed = reduce_send[stages] * grad_scale
    eye = (
        lax.broadcasted_iota(jnp.int32, (128, 128), 0)
        == lax.broadcasted_iota(jnp.int32, (128, 128), 1)
    )
    turned = lax.dot_general(
        jnp.where(eye, 1.0, 0.0),
        summed,
        (((1,), (1,)), ((), ())),
        preferred_element_type=F32,
        precision=lax.Precision.HIGHEST,
    )
    grad_conv_out[...] = summed[:, 0 : conv_weight.shape[1]]
    grad_conv_bias_out[...] = turned[LANE_BIAS : LANE_BIAS + 1]
    grad_mix_out[...] = turned[LANE_MIX : LANE_MIX + hidden]
    grad_mix_bias_out[...] = turned[LANE_MIX_BIAS : LANE_MIX_BIAS + 1]
    grad_out_out[...] = turned[LANE_OUT : LANE_OUT + 1]

    store(4, grad_conv_out, grad_conv_out_hbm)
    store(5, grad_conv_bias_out, grad_conv_bias_out_hbm)
    store(6, grad_mix_out, grad_mix_out_hbm)
    store(7, grad_mix_bias_out, grad_mix_bias_out_hbm)
    store(8, grad_out_out, grad_out_out_hbm)

    for turn in range(NSTEP):
        for field in range(2):
            field_pair(turn, field)[2]()
    for channel in range(2):
        bf_pair(channel)[2]()
    spread_pair[2]()
    for stage in range(stages):
        reduce_copy(stage).wait_send()
    for copy in stores:
        copy.wait()


def hand_over(*refs):
    count = len(refs) // 2
    sem = refs[-1]
    copies = [
        pltpu.make_async_copy(refs[index], refs[count + index], sem.at[index])
        for index in range(count)
    ]
    for copy in copies:
        copy.start()
    for copy in copies:
        copy.wait()


def on_device(
    courant,
    wave_level,
    wave_above,
    adjoint_level,
    adjoint_above,
    residual_data,
    wavelet,
    checkpoint_step,
    source_cells,
    receiver_cells,
    conv_weight,
    conv_bias,
    mix_weight,
    mix_bias,
    out_weight,
    update_cotangent,
):
    n = lax.axis_size("slab")
    planes, nx, ny = courant.shape
    taps, hidden = conv_weight.shape
    receivers = receiver_cells.shape[1]
    stages = n.bit_length() - 1
    grad_scale = float(n * planes * nx * ny) ** (-0.5)
    grid = (planes, nx, ny)
    tall = RB * hidden
    wide = (RB + 2) * SR
    hbm = pl.BlockSpec(memory_space=pltpu.HBM)
    consts = constants(taps, hidden)
    operands = (
        checkpoint_step,
        courant,
        wave_level,
        wave_above,
        adjoint_level,
        adjoint_above,
        residual_data,
        wavelet[None],
        source_cells,
        receiver_cells,
        conv_weight.T,
        conv_bias[None],
        mix_weight,
        mix_bias[None],
        out_weight[None],
        update_cotangent,
        *consts,
    )
    kept = operands[1:2] + operands[6:]
    out_shape = (
        jax.ShapeDtypeStruct(grid, F32),
        jax.ShapeDtypeStruct(grid, F32),
        jax.ShapeDtypeStruct(grid, F32),
        jax.ShapeDtypeStruct(grid, F32),
        jax.ShapeDtypeStruct((hidden, taps), F32),
        jax.ShapeDtypeStruct((1, hidden), F32),
        jax.ShapeDtypeStruct((hidden, hidden), F32),
        jax.ShapeDtypeStruct((1, hidden), F32),
        jax.ShapeDtypeStruct((1, hidden), F32),
    )
    outs = pl.pallas_call(
        functools.partial(kernel, n, grad_scale),
        out_shape=out_shape,
        in_specs=[hbm] * len(operands),
        out_specs=(hbm,) * 9,
        scratch_shapes=[
            pltpu.VMEM((NSTEP + 1,) + grid, F32),
            pltpu.VMEM((NSTEP + 1,) + grid, F32),
            pltpu.VMEM((NSTEP,) + grid, F32),
            pltpu.VMEM((NSTEP, 2, 2, nx, ny), F32),
            pltpu.VMEM((ny, receivers), BF16),
            pltpu.VMEM((planes, ny // 128, (nx + 2) * SR, 128), F32),
            pltpu.VMEM((2,) + grid, BF16),
            pltpu.VMEM((2, 2, nx, ny), BF16),
            pltpu.VMEM(grid, F32),
            pltpu.VMEM((tall, wide), BF16),
            pltpu.VMEM((tall, tall), BF16),
            pltpu.VMEM((tall, tall), BF16),
            pltpu.VMEM(((RB + 2) * QR, tall), BF16),
            pltpu.VMEM((tall, RB), BF16),
            pltpu.VMEM((planes, ny // 128, (nx + 2) * QR, 128), F32),
            pltpu.VMEM((tall, wide), F32),
            pltpu.VMEM((tall, tall), F32),
            pltpu.VMEM((2, tall, RB), F32),
            pltpu.VMEM((2, nx, ny), F32),
            pltpu.VMEM((2, nx, ny), F32),
            pltpu.VMEM((stages + 1, hidden, 128), F32),
            pltpu.VMEM((max(stages, 1), hidden, 128), F32),
            pltpu.SemaphoreType.DMA((EXCH_COUNT, 2)),
            pltpu.SemaphoreType.DMA((EXCH_COUNT, 2)),
            pltpu.SemaphoreType.DMA((max(stages, 1),)),
            pltpu.SemaphoreType.DMA((max(stages, 1),)),
            pltpu.SemaphoreType.DMA((len(operands),)),
            pltpu.SemaphoreType.DMA((9,)),
        ]
        + [pltpu.VMEM(out_shape[index].shape, F32) for index in range(9) if index != 2]
        + [
            pltpu.SMEM((1,), jnp.int32),
        ]
        + [pltpu.VMEM(array.shape, array.dtype) for array in kept],
        compiler_params=pltpu.CompilerParams(
            collective_id=0, has_side_effects=True, vmem_limit_bytes=VMEM_LIMIT
        ),
    )(*operands)
    outs = pl.pallas_call(
        hand_over,
        out_shape=tuple(jax.ShapeDtypeStruct(array.shape, array.dtype) for array in outs),
        in_specs=[hbm] * len(outs),
        out_specs=(hbm,) * len(outs),
        scratch_shapes=[pltpu.SemaphoreType.DMA((len(outs),))],
        compiler_params=pltpu.CompilerParams(vmem_limit_bytes=VMEM_LIMIT),
    )(*outs)
    return outs[:4] + (outs[4].T, outs[5][0], outs[6], outs[7][0], outs[8][0])


def solution(mesh):
    slabs = P(("grp", "slab"), None, None)
    return jax.shard_map(
        on_device,
        mesh=mesh,
        in_specs=(slabs,) * 5
        + (P(None, "grp"), P("grp"), P("grp"), P(None, "grp"), P(None, "grp"))
        + (P(),) * 5
        + (slabs,),
        out_specs=(slabs,) * 4 + (P("grp", None), P("grp"), P("grp", None), P("grp"), P("grp")),
        check_vma=False,
    )
```
